256 devices in a mesh: row: 32 (over z, x_lo, core), col: 8 (over y, x_hi).
Axes of the slice: x: 4 (x_hi: 2, x_lo: 2; x = x_hi * 2 + x_lo), y: 4, z: 8, core: 2. Of those that a mesh axis runs over, the one named last changes fastest.
Arguments:
- x_state: float32 [64, 64, 128, 32], P('row', 'col'), may hold values from -6 to 6
- langevin_noise: float32 [64, 64, 128, 32], P('row', 'col'), may hold values from -6 to 6
- observed: float32 [32768], P('row'), may hold values from -6 to 6
- data_weight: float32 [32768], P('row'), may hold values from 0.5 to 2
- sens_tiles: bfloat16 [32, 8, 48, 128, 128], P('row', 'col'), may hold values from -0.109375 to 0.109375
- tile_rows: int32 [32, 8, 48], P('row', 'col'), may hold values from 0 to 7
- tile_cols: int32 [32, 8, 48], P('row', 'col'), may hold values from 0 to 511
- counts: int32 [32, 8], P('row', 'col'), may hold values from 6 to 48, as said below
Outputs:
- x_next: float32 [64, 64, 128, 32], P('row', 'col')
The draws below stay inside these ranges and needn't reach their ends.
Inputs may be any that keep to these rules, and one draw needn't show every extreme that they name: Only the first counts[r, c] slots of a device hold tiles of G; at least one device uses all 48 slots, the others 48, 24, 12 or 6.
All inputs are finite; a program needn't handle non-finite values.
Results may differ from the reference program's by a relative error of at most 0.0009.
Values may be sent and summed in bfloat16 or wider, within the bound.
No kernel may reach another device: no remote copies, remote signals or barrier semaphores. Data moves between devices by JAX's collectives and lax.ppermute only.
A program may use at most 128 MiB of HBM per device.

```python
import math
import jax
import jax.numpy as jnp
from jax import lax

TILE = 128
CHAINS = 32
RB_DEV = 8
SLOTS = 48
SX = 8
ITERS = 3
NY = 64
NX = 64
NZ = 128
ROWS = 32768
N_ROW = 32
N_COL = 8


def draw_counts(key, part):
    key = jax.random.fold_in(key, 7)
    level_key, full_key = jax.random.split(key)
    levels = jax.random.randint(level_key, (N_ROW * N_COL,), 0, 4)
    divisor = jnp.left_shift(jnp.ones_like(levels), levels)
    filled = SLOTS // divisor
    fullest = jax.random.randint(full_key, (), 0, N_ROW * N_COL)
    filled = filled.at[fullest].set(SLOTS)
    return filled.reshape(N_ROW, N_COL).astype(jnp.int32)


def with_ends(drawn, key, smallest, top_value):
    shape = drawn.shape
    place = [jax.random.randint(jax.random.fold_in(key, axis), (), 0, shape[axis]) for axis in range(len(shape))]
    drawn = drawn.at[tuple(place)].set(smallest)
    longest = shape.index(max(shape))
    place[longest] = (place[longest] + 1) % shape[longest]
    return drawn.at[tuple(place)].set(top_value)


def level_of(own_key, extent, cuts, low, top_value):
    level = 1.0
    for dim, parts in cuts:
        draws = jax.random.uniform(jax.random.fold_in(jax.random.fold_in(own_key, 6), dim), (parts,), jnp.float32, low / len(cuts), top_value / len(cuts))
        level = level * jnp.repeat(jnp.exp(draws), extent[dim] // parts).reshape((-1,) + (1,) * (len(extent) - 1 - dim))
    return level


def scatter_about(key, shape, width, bound, cuts=(), kind=jnp.bfloat16):
    factor_of = level_of(key, shape, cuts, -0.22, 0.18) if cuts else 1.0
    entries = jax.random.normal(key, shape, jnp.float32) * width * factor_of
    return jnp.minimum(jnp.maximum(entries, -bound), bound).astype(kind)


def setup_inputs(seed: int = 0) -> dict:
    seeds = jax.random.split(jax.random.key(seed), 9)
    x_state = scatter_about(seeds[0], (NY, NX, NZ, CHAINS), 1.0, 6.0, ((0, 32), (1, 8)), jnp.float32)
    langevin_noise = scatter_about(seeds[1], (NY, NX, NZ, CHAINS), 1.0, 6.0, ((0, 32), (1, 8)), jnp.float32)
    observed = scatter_about(seeds[2], (ROWS,), 1.0, 6.0, ((0, 32),), jnp.float32)
    data_weight = jnp.clip(jnp.exp(math.log(2.0) - 1.3862944 * jax.random.uniform(seeds[3], (ROWS,), jnp.float32) ** level_of(seeds[3], (ROWS,), ((0, 32),), -0.2, 0.2)), 0.5, 2.0)
    sens_tiles = scatter_about(seeds[4], (N_ROW, N_COL, SLOTS, TILE, TILE), (TILE * SLOTS * N_COL // (2 * RB_DEV)) ** -0.5, 0.109375, ((0, 32), (1, 8)))
    tile_rows = with_ends(jax.random.randint(seeds[5], (N_ROW, N_COL, SLOTS), 0, RB_DEV), jax.random.fold_in(seeds[5], 1), 0, RB_DEV - 1).astype(jnp.int32)
    tile_cols = with_ends(jax.random.randint(seeds[6], (N_ROW, N_COL, SLOTS), 0, SX * NY), jax.random.fold_in(seeds[6], 1), 0, (SX * NY) - 1).astype(jnp.int32)
    counts = draw_counts(jax.random.fold_in(seeds[8], 71), 0)
    return {"x_state": x_state, "langevin_noise": langevin_noise, "observed": observed, "data_weight": data_weight, "sens_tiles": sens_tiles, "tile_rows": tile_rows, "tile_cols": tile_cols, "counts": counts}


theta_tv = 0.25
tau_dual = 1.0 / (12.0 * 0.25)
step_size = 0.5
moreau = 1.0
noise_scale = math.sqrt(2.0 * step_size)

def forward_diff(field):
    diff_y = jnp.concatenate([field[1:] - field[:-1], jnp.zeros_like(field[:1])], axis=0)
    diff_x = jnp.concatenate([field[:, 1:] - field[:, :-1], jnp.zeros_like(field[:, :1])], axis=1)
    diff_z = jnp.concatenate([field[:, :, 1:] - field[:, :, :-1], jnp.zeros_like(field[:, :, :1])], axis=2)
    return jnp.stack([diff_y, diff_x, diff_z])

def lower_shift(field, axis):
    first = lax.slice_in_dim(field, 0, 1, axis=axis)
    rest = lax.slice_in_dim(field, 0, field.shape[axis] - 1, axis=axis)
    return jnp.concatenate([jnp.zeros_like(first), rest], axis=axis)

def adjoint_diff(dual_field):
    term_y = lower_shift(dual_field[0], 0) - dual_field[0]
    term_x = lower_shift(dual_field[1], 1) - dual_field[1]
    term_z = lower_shift(dual_field[2], 2) - dual_field[2]
    return term_y + term_x + term_z

def tv_prox(anchor):
    dual_field = jnp.zeros((3,) + anchor.shape, jnp.float32)
    for step_index in range(ITERS):
        primal_field = anchor - theta_tv * adjoint_diff(dual_field)
        dual_field = jnp.clip(dual_field + tau_dual * forward_diff(primal_field), -1.0, 1.0)
    return anchor - theta_tv * adjoint_diff(dual_field)

def reference(x_state, langevin_noise, observed, data_weight, sens_tiles, tile_rows, tile_cols, counts):
    device_count = N_ROW * N_COL
    x_low = x_state.astype(jnp.bfloat16)
    slab_values = x_low.reshape(NY, N_COL, SX, NZ, CHAINS).transpose(1, 0, 2, 3, 4).reshape(N_COL, NY * SX, NZ, CHAINS)
    flat_tiles = sens_tiles.reshape(device_count, SLOTS, TILE, TILE)
    flat_rows = tile_rows.reshape(device_count, SLOTS)
    flat_cols = tile_cols.reshape(device_count, SLOTS)
    flat_counts = counts.reshape(device_count)
    device_ids = jnp.arange(device_count, dtype=jnp.int32)
    slot_ids = jnp.arange(SLOTS, dtype=jnp.int32)

    def forward_step(running, scan_items):
        tile_set, row_ids, col_ids, slot_count, device_index = scan_items
        row_index = (device_index // N_COL).astype(jnp.int32)
        col_index = (device_index % N_COL).astype(jnp.int32)
        slab_cells = lax.dynamic_index_in_dim(slab_values, col_index, 0, keepdims=False)
        block_values = slab_cells[col_ids].astype(jnp.float32)
        product = jnp.einsum('sij,sjk->sik', tile_set.astype(jnp.float32), block_values)
        product = product * (slot_ids < slot_count).astype(jnp.float32)[:, None, None]
        partial_value = jax.ops.segment_sum(product, row_ids, num_segments=RB_DEV)
        current = lax.dynamic_index_in_dim(running, row_index, 0, keepdims=False)
        running = lax.dynamic_update_index_in_dim(running, current + partial_value, row_index, 0)
        return (running, None)
    start_sum = jnp.zeros((N_ROW, RB_DEV, TILE, CHAINS), jnp.float32)
    predicted, _ = lax.scan(forward_step, start_sum, (flat_tiles, flat_rows, flat_cols, flat_counts, device_ids))
    observed_rows = observed.reshape(N_ROW, RB_DEV, TILE, 1)
    weight_rows = data_weight.reshape(N_ROW, RB_DEV, TILE, 1)
    residual = (weight_rows * (predicted - observed_rows)).astype(jnp.bfloat16)

    def adjoint_step(running, scan_items):
        tile_set, row_ids, col_ids, slot_count, device_index = scan_items
        row_index = (device_index // N_COL).astype(jnp.int32)
        col_index = (device_index % N_COL).astype(jnp.int32)
        res_block = lax.dynamic_index_in_dim(residual, row_index, 0, keepdims=False)
        res_rows = res_block[row_ids].astype(jnp.float32)
        product = jnp.einsum('sij,sik->sjk', tile_set.astype(jnp.float32), res_rows)
        product = product * (slot_ids < slot_count).astype(jnp.float32)[:, None, None]
        partial_value = jax.ops.segment_sum(product, col_ids, num_segments=NY * SX)
        current = lax.dynamic_index_in_dim(running, col_index, 0, keepdims=False)
        running = lax.dynamic_update_index_in_dim(running, current + partial_value, col_index, 0)
        return (running, None)
    grad_start = jnp.zeros((N_COL, NY * SX, TILE, CHAINS), jnp.float32)
    grad_slabs, _ = lax.scan(adjoint_step, grad_start, (flat_tiles, flat_rows, flat_cols, flat_counts, device_ids))
    gradient = grad_slabs.reshape(N_COL, NY, SX, NZ, CHAINS).transpose(1, 0, 2, 3, 4).reshape(NY, NX, NZ, CHAINS)
    prox_field = tv_prox(x_state)
    return x_state - step_size * gradient - step_size / moreau * (x_state - prox_field) + noise_scale * langevin_noise
```

```python
import functools
import math

import jax
import jax.numpy as jnp
from jax import lax
from jax.experimental import pallas as pl
from jax.experimental.pallas import tpu as pltpu
from jax.sharding import PartitionSpec as P

theta_tv = 0.25
tau_dual = 1.0 / (12.0 * 0.25)
step_size = 0.5
moreau = 1.0
noise_scale = math.sqrt(2.0 * step_size)

F32 = jnp.float32
BF16 = jnp.bfloat16

N_Z = 8
QUAD = 4
N_ROW = N_Z * QUAD
N_COL = 8
OWN_Y = 2
OWN_X = 8
OWN = OWN_Y * OWN_X
PLANE = QUAD * OWN
HALF = PLANE // 2
LINES = N_Z * PLANE
CH = 32
NZ = 128
RB = 8
SLOTS = 48
GROUP = 8
HALO = 3
WIDE_Y = OWN_Y + 2 * HALO
WIDE_X = OWN_X + 2 * HALO
TOP_Y = N_ROW * OWN_Y - 1
TOP_X = N_COL * OWN_X - 1
SENT = HALF + 3 * PLANE

CORE = [(i, i ^ 1) for i in range(N_ROW)]
X_LO = [(i, i ^ 2) for i in range(N_ROW)]
RING = [(i, (i + (QUAD if i % 2 == 0 else -QUAD)) % N_ROW) for i in range(N_ROW)]
QUADS = [[QUAD * z + q for q in range(QUAD)] for z in range(N_Z)]

VMEM = pl.BlockSpec(memory_space=pltpu.VMEM)
SMEM = pl.BlockSpec(memory_space=pltpu.SMEM)


def over_row(value, pairs):
    return lax.ppermute(value, "row", pairs)


def over_col(value, pairs):
    return lax.ppermute(value, "col", pairs)


def own_half(value, pick):
    half = value.shape[0] // 2
    return jnp.where(pick == 0, value[:half], value[half:])


def params():
    return pltpu.CompilerParams(vmem_limit_bytes=48 * 2**20)


def forward_kernel(place, rows, cols, count, tiles, own, *rest):
    arrived, out, field, total = rest[:-3], rest[-3], rest[-2], rest[-1]
    z = place[0]
    core = place[1]
    up = 1 - 2 * core

    def keep(ref, steps, half):
        plane = lax.rem(z + steps + 2 * N_Z, N_Z)
        field[pl.ds(plane * PLANE + half * HALF, HALF)] = ref[...]

    field[pl.ds(z * PLANE, PLANE)] = own[...]
    for step in range(1, 5):
        keep(arrived[step - 1], -step * up, core)
        keep(arrived[step + 3], step * up, 1 - core)
    for step in range(1, 4):
        keep(arrived[step + 7], -step * up, 1 - core)
        keep(arrived[step + 10], step * up, core)
    total[...] = jnp.zeros_like(total)
    used = count[0]

    def group(index, carry):
        terms = []
        for u in range(GROUP):
            slot = index * GROUP + u
            term = lax.dot_general(
                field[cols[slot]], tiles[slot], (((1,), (1,)), ((), ())), preferred_element_type=F32
            )
            terms.append(jnp.where(slot < used, term, 0.0))
        for u in range(GROUP):
            total[rows[index * GROUP + u]] += terms[u]
        return carry

    lax.fori_loop(0, (used + GROUP - 1) // GROUP, group, 0)
    out[...] = total[...].astype(BF16)


def forward(place, rows, cols, count, tiles, own, arrived):
    return pl.pallas_call(
        forward_kernel,
        out_shape=jax.ShapeDtypeStruct((RB, CH, NZ), BF16),
        in_specs=[SMEM] * 4 + [VMEM] * (2 + len(arrived)),
        out_specs=VMEM,
        scratch_shapes=[pltpu.VMEM((LINES, CH, NZ), BF16), pltpu.VMEM((RB, CH, NZ), F32)],
        compiler_params=params(),
        cost_estimate=pl.CostEstimate(
            flops=2 * SLOTS * NZ * NZ * CH, bytes_accessed=12 * 2**20, transcendentals=0
        ),
        name="forward_tiles",
    )(place, rows, cols, count, tiles, own, *arrived)


def adjoint_kernel(
    place, rows, cols, count, tiles, observed, weight, *rest
):
    parts, (send, mine, own, residual, total, first) = rest[:4], rest[4:]
    z = place[0]
    core = place[1]
    used = count[0]
    for b in range(RB):
        predicted = parts[0][b].astype(F32)
        for part in parts[1:]:
            predicted = predicted + part[b].astype(F32)
        residual[b] = (weight[pl.ds(b, 1), :] * (predicted - observed[pl.ds(b, 1), :])).astype(BF16)
    total[...] = jnp.zeros_like(total)
    send[...] = jnp.zeros_like(send)
    mine[...] = jnp.zeros_like(mine)
    own[...] = jnp.zeros_like(own)

    def mark(index, carry):
        slot = used - 1 - index
        first[cols[slot]] = slot
        return carry

    lax.fori_loop(0, used, mark, 0)

    def group(index, carry):
        terms = []
        for u in range(GROUP):
            slot = index * GROUP + u
            term = lax.dot_general(
                residual[rows[slot]], tiles[slot], (((1,), (0,)), ((), ())), preferred_element_type=F32
            )
            terms.append(term)
        for u in range(GROUP):
            slot = index * GROUP + u

            @pl.when(slot < used)
            def _():
                total[first[cols[slot]]] += terms[u]

        return carry

    lax.fori_loop(0, (used + GROUP - 1) // GROUP, group, 0)

    def place_line(slot, carry):
        line = cols[slot]
        value = total[first[line]].astype(BF16)
        plane = line // PLANE
        inner = lax.rem(line, PLANE)
        half = inner // HALF
        away = lax.rem(plane - z + N_Z, N_Z)
        carrier = jnp.where(away == 4, half, jnp.where(away < 4, 0, 1))
        steps = jnp.where(carrier == 0, away, N_Z - away)
        where = jnp.where(half == carrier, 0, HALF) + lax.rem(inner, HALF)
        where = jnp.where(steps == 4, where, HALF + (3 - steps) * PLANE + where)

        @pl.when(away == 0)
        def _():
            own[inner] = value

        @pl.when((away != 0) & (carrier == core))
        def _():
            mine[where] = value

        @pl.when((away != 0) & (carrier != core))
        def _():
            send[where] = value

        return carry

    lax.fori_loop(0, used, place_line, 0)


def adjoint(place, rows, cols, count, tiles, observed, weight, parts):
    return pl.pallas_call(
        adjoint_kernel,
        out_shape=[
            jax.ShapeDtypeStruct((SENT, CH, NZ), BF16),
            jax.ShapeDtypeStruct((SENT, CH, NZ), BF16),
            jax.ShapeDtypeStruct((PLANE, CH, NZ), BF16),
        ],
        in_specs=[SMEM] * 4 + [VMEM] * (3 + len(parts)),
        out_specs=[VMEM] * 3,
        scratch_shapes=[
            pltpu.VMEM((RB, CH, NZ), BF16),
            pltpu.VMEM((SLOTS, CH, NZ), F32),
            pltpu.SMEM((LINES,), jnp.int32),
        ],
        compiler_params=params(),
        cost_estimate=pl.CostEstimate(
            flops=2 * SLOTS * NZ * NZ * CH, bytes_accessed=12 * 2**20, transcendentals=0
        ),
        name="adjoint_tiles",
    )(place, rows, cols, count, tiles, observed, weight, *parts)


def prox_kernel(start, wide, low, high, anchor, noise, out, field, primal, dual_y, dual_x, dual_z):
    y0 = start[0]
    x0 = start[1]
    lane = lax.broadcasted_iota(jnp.int32, (CH, NZ), 1)
    not_first = lane > 0
    not_last = lane < NZ - 1

    def load_line(y, carry):
        for x in range(OWN_X):
            field[y, HALO + x] = wide[y, x].astype(F32)
        for x in range(HALO):
            field[y, x] = low[y, x].astype(F32)
            field[y, HALO + OWN_X + x] = high[y, x].astype(F32)
        return carry

    lax.fori_loop(0, WIDE_Y, load_line, 0)
    for y in range(OWN_Y):
        for x in range(OWN_X):
            field[HALO + y, HALO + x] = anchor[y, x]

    def primal_at(y, x):
        along_z = dual_z[y, x]
        lower_z = jnp.where(not_first, pltpu.roll(along_z, 1, 1), 0.0)
        term = (dual_y[y - 1, x] - dual_y[y, x]) + (dual_x[y, x - 1] - dual_x[y, x]) + (lower_z - along_z)
        return field[y, x] - theta_tv * term

    for step in range(3):
        source = field if step == 0 else primal
        if step:

            def primal_line(y, carry, step=step):
                for x in range(step, WIDE_X - step):
                    primal[y, x] = primal_at(y, x)
                return carry

            lax.fori_loop(step, WIDE_Y - step, primal_line, 0)

        def dual_line(y, carry, step=step, source=source):
            line = y0 + y
            rate_y = jnp.where((line >= 0) & (line < TOP_Y), tau_dual, 0.0)
            for x in range(step, WIDE_X - 1 - step):
                plane = x0 + x
                rate_x = jnp.where((plane >= 0) & (plane < TOP_X), tau_dual, 0.0)
                here = source[y, x]
                diff_y = rate_y * (source[y + 1, x] - here)
                diff_x = rate_x * (source[y, x + 1] - here)
                diff_z = jnp.where(not_last, tau_dual * (pltpu.roll(here, NZ - 1, 1) - here), 0.0)
                if step:
                    diff_y = dual_y[y, x] + diff_y
                    diff_x = dual_x[y, x] + diff_x
                    diff_z = dual_z[y, x] + diff_z
                dual_y[y, x] = jnp.clip(diff_y, -1.0, 1.0)
                dual_x[y, x] = jnp.clip(diff_x, -1.0, 1.0)
                dual_z[y, x] = jnp.clip(diff_z, -1.0, 1.0)
            return carry

        lax.fori_loop(step, WIDE_Y - 1 - step, dual_line, 0)
    for y in range(OWN_Y):
        for x in range(OWN_X):
            here = field[HALO + y, HALO + x]
            prox = primal_at(HALO + y, HALO + x)
            out[y, x] = here - step_size / moreau * (here - prox) + noise_scale * noise[y, x]


def prox_step(start, wide, low, high, anchor, noise):
    region = pltpu.VMEM((WIDE_Y, WIDE_X, CH, NZ), F32)
    return pl.pallas_call(
        prox_kernel,
        out_shape=jax.ShapeDtypeStruct((OWN_Y, OWN_X, CH, NZ), F32),
        in_specs=[SMEM] + [VMEM] * 5,
        out_specs=VMEM,
        scratch_shapes=[region] * 5,
        compiler_params=params(),
        cost_estimate=pl.CostEstimate(flops=2**24, bytes_accessed=12 * 2**20, transcendentals=0),
        name="tv_prox",
    )(start, wide, low, high, anchor, noise)


def gather_slab(own, core):
    plane = lax.all_gather(own, "row", axis=0, tiled=True, axis_index_groups=QUADS)
    long, short = own_half(plane, core), own_half(plane, 1 - core)
    mine_long, mine_short = [], []
    for step in range(4):
        long = over_row(long, RING)
        mine_long.append(long)
        if step < 3:
            short = over_row(short, RING)
            mine_short.append(short)
    their_long = [over_row(v, CORE) for v in mine_long]
    their_short = [over_row(v, CORE) for v in mine_short]
    return plane, mine_long, their_long, mine_short, their_short


def add(*parts):
    total = parts[0].astype(F32)
    for part in parts[1:]:
        total = total + part.astype(F32)
    return total.astype(BF16)


def scatter_gradient(send, mine, own, x_lo, core):
    came = over_row(send, CORE)

    def chip(start):
        return add(mine[start : start + HALF], came[start : start + HALF])

    long = over_row(chip(0), RING)
    short = over_row(chip(2 * HALF), RING)
    for step in (1, 2):
        long = over_row(add(long, chip((2 * step - 1) * HALF)), RING)
        short = over_row(add(short, chip((2 * step + 2) * HALF)), RING)
    long = over_row(add(long, chip(5 * HALF)), RING)
    low = add(jnp.where(core == 0, long, short), own[:HALF])
    high = add(jnp.where(core == 0, short, long), own[HALF:])
    kept = jnp.where(x_lo == 0, low, high)
    half = add(kept, over_row(jnp.where(x_lo == 0, high, low), X_LO))
    other = over_row(own_half(half, 1 - core), CORE)
    return own_half(half, core).astype(F32) + other.astype(F32)


def body(x_state, langevin_noise, observed, data_weight, sens_tiles, tile_rows, tile_cols, counts):
    row = lax.axis_index("row")
    col = lax.axis_index("col")
    z, x_lo, core = row // QUAD, (row // 2) % 2, row % 2
    place = jnp.stack([z, core]).astype(jnp.int32)
    state = x_state.transpose(0, 1, 3, 2)
    noise = langevin_noise.transpose(0, 1, 3, 2)
    own = state.reshape(OWN, CH, NZ).astype(BF16)
    tiles = sens_tiles[0, 0]
    rows, cols, count = tile_rows[0, 0], tile_cols[0, 0], counts[0]

    plane, mine_long, their_long, mine_short, their_short = gather_slab(own, core)
    part = forward(
        place, rows, cols, count, tiles, plane, mine_long + their_long + mine_short + their_short
    )
    part = add(part, over_col(part, [(i, i ^ 1) for i in range(N_COL)]))
    parts = [part] + [
        over_col(part, [(i, (i + by) % N_COL) for i in range(N_COL)]) for by in (2, 4, 6)
    ]
    send, mine, kept = adjoint(
        place,
        rows,
        cols,
        count,
        tiles,
        observed.reshape(RB, NZ),
        data_weight.reshape(RB, NZ),
        parts,
    )

    below_low = jnp.where(core == 0, mine_long[0], their_long[0])
    below_high = jnp.where(core == 0, mine_short[0], their_short[0])
    above_low = jnp.where(core == 0, their_short[0], mine_short[0])
    above_high = jnp.where(core == 0, their_long[0], mine_long[0])
    near = jnp.concatenate([below_low, below_high, plane, above_low, above_high], axis=0)
    first = PLANE + (row % QUAD) * OWN - HALO * OWN_X
    wide = lax.dynamic_slice_in_dim(near, first, WIDE_Y * OWN_X, 0)
    wide = wide.reshape(WIDE_Y, OWN_X, CH, NZ)
    low = over_col(wide[:, OWN_X - HALO :], [(i, i + 1) for i in range(N_COL - 1)])
    high = over_col(wide[:, :HALO], [(i + 1, i) for i in range(N_COL - 1)])
    start = jnp.stack([row * OWN_Y - HALO, col * OWN_X - HALO]).astype(jnp.int32)
    base = prox_step(start, wide, low, high, state, noise)

    gradient = scatter_gradient(send, mine, kept, x_lo, core)
    out = base - step_size * gradient.reshape(OWN_Y, OWN_X, CH, NZ)
    return out.transpose(0, 1, 3, 2)


def solution(mesh):
    placed = (
        P("row", "col", None, None),
        P("row", "col", None, None),
        P("row"),
        P("row"),
        P("row", "col", None, None, None),
        P("row", "col", None),
        P("row", "col", None),
        P("row", "col"),
    )
    return jax.shard_map(
        body, mesh=mesh, in_specs=placed, out_specs=P("row", "col", None, None), check_vma=False
    )
```

```python
import functools
import math

import jax
import jax.numpy as jnp
from jax import lax
from jax.experimental import pallas as pl
from jax.experimental.pallas import tpu as pltpu
from jax.sharding import PartitionSpec as P

theta_tv = 0.25
tau_dual = 1.0 / (12.0 * 0.25)
step_size = 0.5
moreau = 1.0
noise_scale = math.sqrt(2.0 * step_size)

F32 = jnp.float32
BF16 = jnp.bfloat16

N_Z = 8
QUAD = 4
N_ROW = N_Z * QUAD
N_COL = 8
OWN_Y = 2
OWN_X = 8
OWN = OWN_Y * OWN_X
PLANE = QUAD * OWN
HALF = PLANE // 2
LINES = N_Z * PLANE
CH = 32
NZ = 128
RB = 8
SLOTS = 48
GROUP = 8
HALO = 3
WIDE_Y = OWN_Y + 2 * HALO
WIDE_X = OWN_X + 2 * HALO
TOP_Y = N_ROW * OWN_Y - 1
TOP_X = N_COL * OWN_X - 1
LONG = 2 * OWN
SENT = LONG + 3 * PLANE
FIRST = LONG + PLANE

CORE = [(i, i ^ 1) for i in range(N_ROW)]
X_HI = [(i, i ^ 1) for i in range(N_COL)]
ACROSS = [(i, (i - 1 + 2 * (i % 2)) % N_COL) for i in range(N_COL)]
X_LO = [(i, i ^ 2) for i in range(N_ROW)]
RING = [(i, (i + (QUAD if i % 2 == 0 else -QUAD)) % N_ROW) for i in range(N_ROW)]

CHAINS = ((2, 0), (3, 1))
QUADS = [[QUAD * z + q for q in range(QUAD)] for z in range(N_Z)]
MINE = [(0, steps) for steps in range(1, 5)] + [(1, steps) for steps in range(1, 4)]
PIECES = MINE + [(1 - flip, -steps) for flip, steps in MINE]

ANY = pl.BlockSpec(memory_space=pl.ANY)
VMEM = pl.BlockSpec(memory_space=pltpu.VMEM)
SMEM = pl.BlockSpec(memory_space=pltpu.SMEM)


def over_row(value, pairs):
    return lax.ppermute(value, "row", pairs)


def over_col(value, pairs):
    return lax.ppermute(value, "col", pairs)


def after(value, other):
    return lax.optimization_barrier((value, other))[0]


def params():
    return pltpu.CompilerParams(vmem_limit_bytes=20 * 2**20)


def forward_kernel(place, rows, cols, count, tiles, plane, *rest):
    pieces, (out, wide, near, far, field, total, sems) = rest[: len(PIECES)], rest[len(PIECES) :]
    z = place[0]
    quad = place[1]
    core = quad & 1
    up = 1 - 2 * core
    copies = [pltpu.make_async_copy(plane, field.at[pl.ds(z * PLANE, PLANE)], sems.at[len(PIECES)])]
    for i, ((flip, steps), piece) in enumerate(zip(PIECES, pieces)):
        from_plane = lax.rem(z - steps * up + 2 * N_Z, N_Z)
        half = core if flip == 0 else 1 - core
        there = field.at[pl.ds(from_plane * PLANE + half * HALF, HALF)]
        copies.append(pltpu.make_async_copy(piece, there, sems.at[i]))
    for copy in copies:
        copy.start()
    for copy in copies:
        copy.wait()
    total[...] = jnp.zeros_like(total)
    used = count[0]

    def group(index, carry):
        terms = []
        for u in range(GROUP):
            slot = index * GROUP + u
            term = lax.dot_general(
                field[cols[slot]], tiles[slot], (((1,), (1,)), ((), ())), preferred_element_type=F32
            )
            terms.append(jnp.where(slot < used, term, 0.0))
        for u in range(GROUP):
            total[rows[index * GROUP + u]] += terms[u]
        return carry

    lax.fori_loop(0, (used + GROUP - 1) // GROUP, group, 0)
    out[...] = total[...].astype(BF16)
    to_near = jnp.where(place[2] == 0, OWN_X - HALO, 0)
    to_far = OWN_X - HALO - to_near
    for y in range(WIDE_Y):
        line = lax.rem((z * QUAD + quad) * OWN_Y - HALO + y + N_ROW * OWN_Y, N_ROW * OWN_Y) * OWN_X
        wide[y] = field[pl.ds(line, OWN_X)]
        near[y] = field[pl.ds(line + to_near, HALO)]
        far[y] = field[pl.ds(line + to_far, HALO)]


def forward(place, rows, cols, count, tiles, plane, pieces):
    return pl.pallas_call(
        forward_kernel,
        out_shape=[
            jax.ShapeDtypeStruct((RB, CH, NZ), BF16),
            jax.ShapeDtypeStruct((WIDE_Y, OWN_X, CH, NZ), BF16),
            jax.ShapeDtypeStruct((WIDE_Y, HALO, CH, NZ), BF16),
            jax.ShapeDtypeStruct((WIDE_Y, HALO, CH, NZ), BF16),
        ],
        in_specs=[SMEM] * 4 + [VMEM] + [ANY] * (1 + len(pieces)),
        out_specs=[VMEM] * 4,
        scratch_shapes=[
            pltpu.VMEM((LINES, CH, NZ), BF16),
            pltpu.VMEM((RB, CH, NZ), F32),
            pltpu.SemaphoreType.DMA((1 + len(pieces),)),
        ],
        compiler_params=params(),
        cost_estimate=pl.CostEstimate(
            flops=2 * SLOTS * NZ * NZ * CH, bytes_accessed=12 * 2**20, transcendentals=0
        ),
        name="forward_tiles",
    )(place, rows, cols, count, tiles, plane, *pieces)


def adjoint_kernel(
    place, rows, cols, count, tiles, observed, weight, *rest
):
    parts, (soon, later, mine, own, residual, total, first) = rest[:4], rest[4:]
    z = place[0]
    quad = place[1]
    core = quad & 1
    used = count[0]
    for b in range(RB):
        predicted = parts[0][b].astype(F32)
        for part in parts[1:]:
            predicted = predicted + part[b].astype(F32)
        residual[b] = (weight[pl.ds(b, 1), :] * (predicted - observed[pl.ds(b, 1), :])).astype(BF16)
    total[...] = jnp.zeros_like(total)
    soon[...] = jnp.zeros_like(soon)
    later[...] = jnp.zeros_like(later)
    mine[...] = jnp.zeros_like(mine)
    own[...] = jnp.zeros_like(own)

    def mark(index, carry):
        slot = used - 1 - index
        first[cols[slot]] = slot
        return carry

    lax.fori_loop(0, used, mark, 0)

    def group(index, carry):
        terms = []
        for u in range(GROUP):
            slot = index * GROUP + u
            term = lax.dot_general(
                residual[rows[slot]], tiles[slot], (((1,), (0,)), ((), ())), preferred_element_type=F32
            )
            terms.append(term)
        for u in range(GROUP):
            slot = index * GROUP + u

            @pl.when(slot < used)
            def _():
                total[first[cols[slot]]] += terms[u]

        return carry

    lax.fori_loop(0, (used + GROUP - 1) // GROUP, group, 0)

    def place_line(slot, carry):
        line = cols[slot]
        value = total[first[line]].astype(BF16)
        away = lax.rem(line // PLANE - z + N_Z, N_Z)
        other = lax.rem(line // OWN, QUAD)
        inner = lax.rem(line, OWN)
        carrier = jnp.where(away == 4, other & 1, jnp.where(away < 4, 0, 1))
        steps = jnp.where(carrier == 0, away, N_Z - away)
        turn = 2 * ((other & 1) ^ carrier) + 1 - ((other // 2) ^ (quad // 2))
        where = jnp.where(steps == 4, 0, LONG + (3 - steps) * PLANE) + turn * OWN + inner
        own_place = (2 * ((other & 1) ^ core) + 1 - ((other // 2) ^ (quad // 2))) * OWN + inner

        @pl.when(away == 0)
        def _():
            own[own_place] = value

        @pl.when((away != 0) & (carrier == core))
        def _():
            mine[where] = value

        @pl.when((away != 0) & (carrier != core) & (where < FIRST))
        def _():
            soon[where] = value

        @pl.when((away != 0) & (carrier != core) & (where >= FIRST))
        def _():
            later[where - FIRST] = value

        return carry

    lax.fori_loop(0, used, place_line, 0)


def adjoint(place, rows, cols, count, tiles, observed, weight, parts):
    return pl.pallas_call(
        adjoint_kernel,
        out_shape=[
            jax.ShapeDtypeStruct((FIRST, CH, NZ), BF16),
            jax.ShapeDtypeStruct((SENT - FIRST, CH, NZ), BF16),
            jax.ShapeDtypeStruct((SENT, CH, NZ), BF16),
            jax.ShapeDtypeStruct((PLANE, CH, NZ), BF16),
        ],
        in_specs=[SMEM] * 4 + [VMEM] * (3 + len(parts)),
        out_specs=[VMEM] * 4,
        scratch_shapes=[
            pltpu.VMEM((RB, CH, NZ), BF16),
            pltpu.VMEM((SLOTS, CH, NZ), F32),
            pltpu.SMEM((LINES,), jnp.int32),
        ],
        compiler_params=params(),
        cost_estimate=pl.CostEstimate(
            flops=2 * SLOTS * NZ * NZ * CH, bytes_accessed=12 * 2**20, transcendentals=0
        ),
        name="adjoint_tiles",
    )(place, rows, cols, count, tiles, observed, weight, *parts)


def prox_kernel(start, wide, near, far, anchor, noise, out, field, primal, dual_y, dual_x, dual_z):
    y0 = start[0]
    x0 = start[1]
    above = jnp.where(start[2] == 0, HALO + OWN_X, 0)
    below = HALO + OWN_X - above
    lane = lax.broadcasted_iota(jnp.int32, (CH, NZ), 1)
    not_first = lane > 0
    not_last = lane < NZ - 1

    def load_line(y, carry):
        for x in range(OWN_X):
            field[y, HALO + x] = wide[y, x].astype(F32)
        for x in range(HALO):
            field[y, above + x] = near[y, x].astype(F32)
            field[y, below + x] = far[y, x].astype(F32)
        return carry

    lax.fori_loop(0, WIDE_Y, load_line, 0)
    for y in range(OWN_Y):
        for x in range(OWN_X):
            field[HALO + y, HALO + x] = anchor[y, x]

    def primal_at(y, x):
        along_z = dual_z[y, x]
        lower_z = jnp.where(not_first, pltpu.roll(along_z, 1, 1), 0.0)
        term = (dual_y[y - 1, x] - dual_y[y, x]) + (dual_x[y, x - 1] - dual_x[y, x]) + (lower_z - along_z)
        return field[y, x] - theta_tv * term

    for step in range(3):
        source = field if step == 0 else primal
        if step:

            def primal_line(y, carry, step=step):
                for x in range(step, WIDE_X - step):
                    primal[y, x] = primal_at(y, x)
                return carry

            lax.fori_loop(step, WIDE_Y - step, primal_line, 0)

        def dual_line(y, carry, step=step, source=source):
            line = y0 + y
            rate_y = jnp.where((line >= 0) & (line < TOP_Y), tau_dual, 0.0)
            for x in range(step, WIDE_X - 1 - step):
                plane = x0 + x
                rate_x = jnp.where((plane >= 0) & (plane < TOP_X), tau_dual, 0.0)
                here = source[y, x]
                diff_y = rate_y * (source[y + 1, x] - here)
                diff_x = rate_x * (source[y, x + 1] - here)
                diff_z = jnp.where(not_last, tau_dual * (pltpu.roll(here, NZ - 1, 1) - here), 0.0)
                if step:
                    diff_y = dual_y[y, x] + diff_y
                    diff_x = dual_x[y, x] + diff_x
                    diff_z = dual_z[y, x] + diff_z
                dual_y[y, x] = jnp.clip(diff_y, -1.0, 1.0)
                dual_x[y, x] = jnp.clip(diff_x, -1.0, 1.0)
                dual_z[y, x] = jnp.clip(diff_z, -1.0, 1.0)
            return carry

        lax.fori_loop(step, WIDE_Y - 1 - step, dual_line, 0)
    for y in range(OWN_Y):
        for x in range(OWN_X):
            here = field[HALO + y, HALO + x]
            prox = primal_at(HALO + y, HALO + x)
            out[y, x] = here - step_size / moreau * (here - prox) + noise_scale * noise[y, x]


def prox_step(start, wide, near, far, anchor, noise):
    region = pltpu.VMEM((WIDE_Y, WIDE_X, CH, NZ), F32)
    return pl.pallas_call(
        prox_kernel,
        out_shape=jax.ShapeDtypeStruct((OWN_Y, OWN_X, CH, NZ), F32),
        in_specs=[SMEM] + [VMEM] * 5,
        out_specs=VMEM,
        scratch_shapes=[region] * 5,
        compiler_params=params(),
        cost_estimate=pl.CostEstimate(flops=2**24, bytes_accessed=12 * 2**20, transcendentals=0),
        name="tv_prox",
    )(start, wide, near, far, anchor, noise)


def own_half(value, pick):
    half = value.shape[0] // 2
    return jnp.where(pick == 0, value[:half], value[half:])


def gather_slab(own, core):
    plane = lax.all_gather(own, "row", axis=0, tiled=True, axis_index_groups=QUADS)
    chains = [own_half(plane, core), own_half(plane, 1 - core)]
    mine = {}
    for steps in range(1, 5):
        for flip in range(2 if steps < 4 else 1):
            chains[flip] = over_row(chains[flip], RING)
            mine[flip, steps] = chains[flip]
    theirs = [over_row(mine[key], CORE) for key in MINE]
    return [plane] + [mine[key] for key in MINE] + theirs


def add(*parts):
    total = parts[0].astype(F32)
    for part in parts[1:]:
        total = total + part.astype(F32)
    return total.astype(BF16)


def scatter_gradient(soon, later, mine, own, chains, beside):
    came_soon = over_row(soon, CORE)
    came_later = over_row(later, CORE)
    turns = {2: 0, 0: 1, 3: 2, 1: 3}

    def chip(steps, sides, *more):
        start = (0 if steps == 4 else LONG + (3 - steps) * PLANE) + turns[sides[0]] * OWN
        size = len(sides) * OWN
        came = came_soon if start < FIRST else came_later
        first = start if start < FIRST else start - FIRST
        return add(mine[start : start + size], came[first : first + size], *more)

    ring = {}
    last = None
    long, short = chains
    for steps, sides in ((4, long), (3, short), (3, long), (2, short), (2, long), (1, short), (1, long)):
        more = [after(ring[sides], last)] if sides in ring else []
        last = chip(steps, sides, *more)
        ring[sides] = over_row(last, RING)
    pieces = {}
    for sides in chains:
        for i, side in enumerate(sides):
            turn = turns[side]
            pieces[side] = (ring[sides][i * OWN : (i + 1) * OWN], own[turn * OWN : (turn + 1) * OWN])
    give = [add(*pieces[2]), add(*pieces[3])]
    got = [over_row(v, X_LO) for v in give]
    result = beside(give)
    got = after(got, result)
    other = over_row(add(*pieces[1], got[1]), CORE)
    return [*pieces[0], got[0], other], result


def body(x_state, langevin_noise, observed, data_weight, sens_tiles, tile_rows, tile_cols, counts):
    row = lax.axis_index("row")
    col = lax.axis_index("col")
    place = jnp.stack([row // QUAD, row % QUAD, col % 2]).astype(jnp.int32)
    start = jnp.stack([row * OWN_Y - HALO, col * OWN_X - HALO, col % 2]).astype(jnp.int32)
    state = x_state.transpose(0, 1, 3, 2)
    noise = langevin_noise.transpose(0, 1, 3, 2)
    own = after(state, (place, start)).reshape(OWN, CH, NZ).astype(BF16)
    tiles = sens_tiles[0, 0]
    rows, cols, count = tile_rows[0, 0], tile_cols[0, 0], counts[0]

    plane, *pieces = gather_slab(own, row % 2)
    part, wide, to_near, to_far = forward(place, rows, cols, count, tiles, plane, pieces)
    came = over_col(part, X_HI)
    near = over_col(to_near, X_HI)
    part = add(part, came)
    parts = [part] + [
        over_col(part, [(i, (i + by) % N_COL) for i in range(N_COL)]) for by in (2, 4, 6)
    ]
    far = over_col(after(to_far, part), ACROSS)
    parts[0] = after(part, (near, far))
    soon, later, mine, kept = adjoint(
        place,
        rows,
        cols,
        count,
        tiles,
        observed.reshape(RB, NZ),
        data_weight.reshape(RB, NZ),
        parts,
    )
    def beside(give):
        return prox_step(start, wide, after(near, give), far, state, noise)

    terms, base = scatter_gradient(soon, later, mine, kept, CHAINS, beside)
    gradient = sum(v.astype(F32) for v in terms)
    out = base - step_size * gradient.reshape(OWN_Y, OWN_X, CH, NZ)
    return out.transpose(0, 1, 3, 2)


def solution(mesh):
    placed = (
        P("row", "col", None, None),
        P("row", "col", None, None),
        P("row"),
        P("row"),
        P("row", "col", None, None, None),
        P("row", "col", None),
        P("row", "col", None),
        P("row", "col"),
    )
    return jax.shard_map(
        body, mesh=mesh, in_specs=placed, out_specs=P("row", "col", None, None), check_vma=False
    )
```

```python
import functools
import math

import jax
import jax.numpy as jnp
from jax import lax
from jax.experimental import pallas as pl
from jax.experimental.pallas import tpu as pltpu
from jax.sharding import PartitionSpec as P

theta_tv = 0.25
tau_dual = 1.0 / (12.0 * 0.25)
step_size = 0.5
moreau = 1.0
noise_scale = math.sqrt(2.0 * step_size)

F32 = jnp.float32
BF16 = jnp.bfloat16

N_Z = 8
QUAD = 4
N_ROW = N_Z * QUAD
N_COL = 8
OWN_Y = 2
OWN_X = 8
OWN = OWN_Y * OWN_X
PLANE = QUAD * OWN
HALF = PLANE // 2
LINES = N_Z * PLANE
CH = 32
NZ = 128
RB = 8
SLOTS = 48
GROUP = 8
HALO = 3
WIDE_Y = OWN_Y + 2 * HALO
WIDE_X = OWN_X + 2 * HALO
TOP_Y = N_ROW * OWN_Y - 1
TOP_X = N_COL * OWN_X - 1
LONG = 2 * OWN
SENT = LONG + 3 * PLANE
FIRST = LONG + PLANE
KEPT = SENT + PLANE

CORE = [(i, i ^ 1) for i in range(N_ROW)]
X_HI = [(i, i ^ 1) for i in range(N_COL)]
ACROSS = [(i, (i - 1 + 2 * (i % 2)) % N_COL) for i in range(N_COL)]
X_LO = [(i, i ^ 2) for i in range(N_ROW)]
RING = [(i, (i + (QUAD if i % 2 == 0 else -QUAD)) % N_ROW) for i in range(N_ROW)]

CHAINS = ((2, 0), (3, 1))
QUADS = [[QUAD * z + q for q in range(QUAD)] for z in range(N_Z)]
MINE = [(0, steps) for steps in range(1, 5)] + [(1, steps) for steps in range(1, 4)]
PIECES = MINE + [(1 - flip, -steps) for flip, steps in MINE]

ANY = pl.BlockSpec(memory_space=pl.ANY)
VMEM = pl.BlockSpec(memory_space=pltpu.VMEM)
SMEM = pl.BlockSpec(memory_space=pltpu.SMEM)


def over_row(value, pairs):
    return lax.ppermute(value, "row", pairs)


def over_col(value, pairs):
    return lax.ppermute(value, "col", pairs)


def after(value, other):
    return lax.optimization_barrier((value, other))[0]


def params():
    return pltpu.CompilerParams(vmem_limit_bytes=20 * 2**20)


def forward_kernel(place, rows, cols, count, tiles, plane, *rest):
    pieces, (out, wide, near, far, field, total, sems) = rest[: len(PIECES)], rest[len(PIECES) :]
    z = place[0]
    quad = place[1]
    core = quad & 1
    up = 1 - 2 * core
    copies = [pltpu.make_async_copy(plane, field.at[pl.ds(z * PLANE, PLANE)], sems.at[len(PIECES)])]
    for i, ((flip, steps), piece) in enumerate(zip(PIECES, pieces)):
        from_plane = lax.rem(z - steps * up + 2 * N_Z, N_Z)
        half = core if flip == 0 else 1 - core
        there = field.at[pl.ds(from_plane * PLANE + half * HALF, HALF)]
        copies.append(pltpu.make_async_copy(piece, there, sems.at[i]))
    for copy in copies:
        copy.start()
    for copy in copies:
        copy.wait()
    total[...] = jnp.zeros_like(total)
    used = count[0]

    def group(index, carry):
        terms = []
        for u in range(GROUP):
            slot = index * GROUP + u
            term = lax.dot_general(
                field[cols[slot]], tiles[slot], (((1,), (1,)), ((), ())), preferred_element_type=F32
            )
            terms.append(jnp.where(slot < used, term, 0.0))
        for u in range(GROUP):
            total[rows[index * GROUP + u]] += terms[u]
        return carry

    lax.fori_loop(0, (used + GROUP - 1) // GROUP, group, 0)
    out[...] = total[...].astype(BF16)
    to_near = jnp.where(place[2] == 0, OWN_X - HALO, 0)
    to_far = OWN_X - HALO - to_near
    for y in range(WIDE_Y):
        line = lax.rem((z * QUAD + quad) * OWN_Y - HALO + y + N_ROW * OWN_Y, N_ROW * OWN_Y) * OWN_X
        wide[y] = field[pl.ds(line, OWN_X)]
        near[y] = field[pl.ds(line + to_near, HALO)]
        far[y] = field[pl.ds(line + to_far, HALO)]


def forward(place, rows, cols, count, tiles, plane, pieces):
    return pl.pallas_call(
        forward_kernel,
        out_shape=[
            jax.ShapeDtypeStruct((RB, CH, NZ), BF16),
            jax.ShapeDtypeStruct((WIDE_Y, OWN_X, CH, NZ), BF16),
            jax.ShapeDtypeStruct((WIDE_Y, HALO, CH, NZ), BF16),
            jax.ShapeDtypeStruct((WIDE_Y, HALO, CH, NZ), BF16),
        ],
        in_specs=[SMEM] * 4 + [VMEM] + [ANY] * (1 + len(pieces)),
        out_specs=[VMEM] * 4,
        scratch_shapes=[
            pltpu.VMEM((LINES, CH, NZ), BF16),
            pltpu.VMEM((RB, CH, NZ), F32),
            pltpu.SemaphoreType.DMA((1 + len(pieces),)),
        ],
        compiler_params=params(),
        cost_estimate=pl.CostEstimate(
            flops=2 * SLOTS * NZ * NZ * CH, bytes_accessed=12 * 2**20, transcendentals=0
        ),
        name="forward_tiles",
    )(place, rows, cols, count, tiles, plane, *pieces)


def adjoint_kernel(
    place, rows, cols, count, tiles, observed, weight, *rest
):
    parts, (soon, later, kept, residual, total, first) = rest[:4], rest[4:]
    z = place[0]
    quad = place[1]
    core = quad & 1
    used = count[0]
    for b in range(RB):
        predicted = parts[0][b].astype(F32)
        for part in parts[1:]:
            predicted = predicted + part[b].astype(F32)
        residual[b] = (weight[pl.ds(b, 1), :] * (predicted - observed[pl.ds(b, 1), :])).astype(BF16)
    total[...] = jnp.zeros_like(total)
    soon[...] = jnp.zeros_like(soon)
    later[...] = jnp.zeros_like(later)
    kept[...] = jnp.zeros_like(kept)

    def mark(index, carry):
        slot = used - 1 - index
        first[cols[slot]] = slot
        return carry

    lax.fori_loop(0, used, mark, 0)
    groups = (used + GROUP - 1) // GROUP

    def group(index, carry):
        terms = []
        for u in range(GROUP):
            slot = index * GROUP + u
            terms.append(
                lax.dot_general(
                    residual[rows[slot]], tiles[slot], (((1,), (0,)), ((), ())), preferred_element_type=F32
                )
            )
        for u in range(GROUP):
            slot = index * GROUP + u
            total[jnp.where(slot < used, first[cols[slot]], SLOTS)] += terms[u]
        return carry

    lax.fori_loop(0, groups, group, 0)

    def place_line(slot):
        line = cols[slot]
        away = lax.rem(line // PLANE - z + N_Z, N_Z)
        other = lax.rem(line // OWN, QUAD)
        inner = lax.rem(line, OWN)
        carrier = jnp.where(away == 4, other & 1, jnp.where(away < 4, 0, 1))
        steps = jnp.where(carrier == 0, away, N_Z - away)
        across = 1 - ((other // 2) ^ (quad // 2))
        where = (2 * ((other & 1) ^ carrier) + across) * OWN + inner
        where = jnp.where(steps == 4, 0, LONG + (3 - steps) * PLANE) + where
        near = SENT + (2 * ((other & 1) ^ core) + across) * OWN + inner
        here = (away == 0) | (carrier == core)
        good = slot < used
        value = total[jnp.where(good, first[line], SLOTS)].astype(BF16)
        kept[jnp.where(good & here, jnp.where(away == 0, near, where), KEPT)] = value
        soon[jnp.where(good & ~here & (where < FIRST), where, FIRST)] = value
        later[jnp.where(good & ~here & (where >= FIRST), where - FIRST, SENT - FIRST)] = value

    def place_group(index, carry):
        for u in range(GROUP):
            place_line(index * GROUP + u)
        return carry

    lax.fori_loop(0, groups, place_group, 0)


def adjoint(place, rows, cols, count, tiles, observed, weight, parts):
    return pl.pallas_call(
        adjoint_kernel,
        out_shape=[
            jax.ShapeDtypeStruct((FIRST + 1, CH, NZ), BF16),
            jax.ShapeDtypeStruct((SENT - FIRST + 1, CH, NZ), BF16),
            jax.ShapeDtypeStruct((KEPT + 1, CH, NZ), BF16),
        ],
        in_specs=[SMEM] * 4 + [VMEM] * (3 + len(parts)),
        out_specs=[VMEM] * 3,
        scratch_shapes=[
            pltpu.VMEM((RB, CH, NZ), BF16),
            pltpu.VMEM((SLOTS + 1, CH, NZ), F32),
            pltpu.SMEM((LINES,), jnp.int32),
        ],
        compiler_params=params(),
        cost_estimate=pl.CostEstimate(
            flops=2 * SLOTS * NZ * NZ * CH, bytes_accessed=12 * 2**20, transcendentals=0
        ),
        name="adjoint_tiles",
    )(place, rows, cols, count, tiles, observed, weight, *parts)


def prox_kernel(start, wide, near, far, anchor, noise, out, field, primal, dual_y, dual_x, dual_z):
    y0 = start[0]
    x0 = start[1]
    above = jnp.where(start[2] == 0, HALO + OWN_X, 0)
    below = HALO + OWN_X - above
    lane = lax.broadcasted_iota(jnp.int32, (CH, NZ), 1)
    not_first = lane > 0
    not_last = lane < NZ - 1

    def load_line(y, carry):
        for x in range(OWN_X):
            field[y, HALO + x] = wide[y, x].astype(F32)
        for x in range(HALO):
            field[y, above + x] = near[y, x].astype(F32)
            field[y, below + x] = far[y, x].astype(F32)
        return carry

    lax.fori_loop(0, WIDE_Y, load_line, 0)
    for y in range(OWN_Y):
        for x in range(OWN_X):
            field[HALO + y, HALO + x] = anchor[y, x]

    def primal_at(y, x):
        along_z = dual_z[y, x]
        lower_z = jnp.where(not_first, pltpu.roll(along_z, 1, 1), 0.0)
        term = (dual_y[y - 1, x] - dual_y[y, x]) + (dual_x[y, x - 1] - dual_x[y, x]) + (lower_z - along_z)
        return field[y, x] - theta_tv * term

    for step in range(3):
        source = field if step == 0 else primal
        if step:

            def primal_line(y, carry, step=step):
                for x in range(step, WIDE_X - step):
                    primal[y, x] = primal_at(y, x)
                return carry

            lax.fori_loop(step, WIDE_Y - step, primal_line, 0)

        def dual_line(y, carry, step=step, source=source):
            line = y0 + y
            rate_y = jnp.where((line >= 0) & (line < TOP_Y), tau_dual, 0.0)
            for x in range(step, WIDE_X - 1 - step):
                plane = x0 + x
                rate_x = jnp.where((plane >= 0) & (plane < TOP_X), tau_dual, 0.0)
                here = source[y, x]
                diff_y = rate_y * (source[y + 1, x] - here)
                diff_x = rate_x * (source[y, x + 1] - here)
                diff_z = jnp.where(not_last, tau_dual * (pltpu.roll(here, NZ - 1, 1) - here), 0.0)
                if step:
                    diff_y = dual_y[y, x] + diff_y
                    diff_x = dual_x[y, x] + diff_x
                    diff_z = dual_z[y, x] + diff_z
                dual_y[y, x] = jnp.clip(diff_y, -1.0, 1.0)
                dual_x[y, x] = jnp.clip(diff_x, -1.0, 1.0)
                dual_z[y, x] = jnp.clip(diff_z, -1.0, 1.0)
            return carry

        lax.fori_loop(step, WIDE_Y - 1 - step, dual_line, 0)
    for y in range(OWN_Y):
        for x in range(OWN_X):
            here = field[HALO + y, HALO + x]
            prox = primal_at(HALO + y, HALO + x)
            out[y, x] = here - step_size / moreau * (here - prox) + noise_scale * noise[y, x]


def prox_step(start, wide, near, far, anchor, noise):
    region = pltpu.VMEM((WIDE_Y, WIDE_X, CH, NZ), F32)
    return pl.pallas_call(
        prox_kernel,
        out_shape=jax.ShapeDtypeStruct((OWN_Y, OWN_X, CH, NZ), F32),
        in_specs=[SMEM] + [VMEM] * 5,
        out_specs=VMEM,
        scratch_shapes=[region] * 5,
        compiler_params=params(),
        cost_estimate=pl.CostEstimate(flops=2**24, bytes_accessed=12 * 2**20, transcendentals=0),
        name="tv_prox",
    )(start, wide, near, far, anchor, noise)


def own_half(value, pick):
    half = value.shape[0] // 2
    return jnp.where(pick == 0, value[:half], value[half:])


def gather_slab(own, core):
    plane = lax.all_gather(own, "row", axis=0, tiled=True, axis_index_groups=QUADS)
    chains = [own_half(plane, core), own_half(plane, 1 - core)]
    mine = {}
    for steps in range(1, 5):
        for flip in range(2 if steps < 4 else 1):
            chains[flip] = over_row(chains[flip], RING)
            mine[flip, steps] = chains[flip]
    theirs = [over_row(mine[key], CORE) for key in MINE]
    return [plane] + [mine[key] for key in MINE] + theirs


def add(*parts):
    total = parts[0].astype(F32)
    for part in parts[1:]:
        total = total + part.astype(F32)
    return total.astype(BF16)


def scatter_gradient(soon, later, kept, chains, beside):
    came_soon = over_row(soon, CORE)
    came_later = over_row(later, CORE)
    turns = {2: 0, 0: 1, 3: 2, 1: 3}

    def chip(steps, sides, *more):
        start = (0 if steps == 4 else LONG + (3 - steps) * PLANE) + turns[sides[0]] * OWN
        size = len(sides) * OWN
        came = came_soon if start < FIRST else came_later
        first = start if start < FIRST else start - FIRST
        return add(kept[start : start + size], came[first : first + size], *more)

    ring = {}
    sent = []
    last = None
    long, short = chains
    for steps, sides in ((4, long), (3, short), (3, long), (2, short), (2, long), (1, short), (1, long)):
        more = [after(ring[sides], last)] if sides in ring else []
        last = chip(steps, sides, *more)
        sent.append(last)
        ring[sides] = over_row(last, RING)

    def terms(sides, side, *order):
        at = sides.index(side) * OWN
        own = SENT + turns[side] * OWN
        brought = after(ring[sides], order) if order else ring[sides]
        return brought[at : at + OWN], kept[own : own + OWN]

    give = add(*terms(short, 3, last))
    other = add(*terms(short, 1, give), over_row(give, X_LO))
    result = beside(sent[2], last)
    give = add(*terms(long, 2, give, result))
    got = over_row(give, X_LO)
    return [*terms(long, 0, give), got, over_row(other, CORE)], result


def body(x_state, langevin_noise, observed, data_weight, sens_tiles, tile_rows, tile_cols, counts):
    row = lax.axis_index("row")
    col = lax.axis_index("col")
    place = jnp.stack([row // QUAD, row % QUAD, col % 2]).astype(jnp.int32)
    start = jnp.stack([row * OWN_Y - HALO, col * OWN_X - HALO, col % 2]).astype(jnp.int32)
    state = x_state.transpose(0, 1, 3, 2)
    noise = langevin_noise.transpose(0, 1, 3, 2)
    own = after(state, (place, start)).reshape(OWN, CH, NZ).astype(BF16)
    tiles = sens_tiles[0, 0]
    rows, cols, count = tile_rows[0, 0], tile_cols[0, 0], counts[0]

    plane, *pieces = gather_slab(own, row % 2)
    part, wide, to_near, to_far = forward(place, rows, cols, count, tiles, plane, pieces)
    came = over_col(part, X_HI)
    near = over_col(to_near, X_HI)
    part = add(part, came)
    parts = [part] + [
        over_col(part, [(i, (i + by) % N_COL) for i in range(N_COL)]) for by in (2, 4, 6)
    ]
    parts[0] = after(part, near)
    soon, later, kept = adjoint(
        place,
        rows,
        cols,
        count,
        tiles,
        observed.reshape(RB, NZ),
        data_weight.reshape(RB, NZ),
        parts,
    )
    def beside(early, last):
        far = over_col(after(to_far, early), ACROSS)
        return prox_step(start, wide, after(near, last), far, state, noise)

    terms, base = scatter_gradient(soon, later, kept, CHAINS, beside)
    gradient = sum(v.astype(F32) for v in terms)
    out = base - step_size * gradient.reshape(OWN_Y, OWN_X, CH, NZ)
    return out.transpose(0, 1, 3, 2)


def solution(mesh):
    placed = (
        P("row", "col", None, None),
        P("row", "col", None, None),
        P("row"),
        P("row"),
        P("row", "col", None, None, None),
        P("row", "col", None),
        P("row", "col", None),
        P("row", "col"),
    )
    return jax.shard_map(
        body, mesh=mesh, in_specs=placed, out_specs=P("row", "col", None, None), check_vma=False
    )
```

```python
import functools
import math

import jax
import jax.numpy as jnp
from jax import lax
from jax.experimental import pallas as pl
from jax.experimental.pallas import tpu as pltpu
from jax.sharding import PartitionSpec as P

theta_tv = 0.25
tau_dual = 1.0 / (12.0 * 0.25)
step_size = 0.5
moreau = 1.0
noise_scale = math.sqrt(2.0 * step_size)

F32 = jnp.float32
BF16 = jnp.bfloat16

N_Z = 8
QUAD = 4
N_ROW = N_Z * QUAD
N_COL = 8
OWN_Y = 2
OWN_X = 8
OWN = OWN_Y * OWN_X
PLANE = QUAD * OWN
HALF = PLANE // 2
LINES = N_Z * PLANE
CH = 32
NZ = 128
RB = 8
SLOTS = 48
GROUP = 8
HALO = 3
WIDE_Y = OWN_Y + 2 * HALO
WIDE_X = OWN_X + 2 * HALO
TOP_Y = N_ROW * OWN_Y - 1
TOP_X = N_COL * OWN_X - 1
LONG = 2 * OWN
SENT = LONG + 3 * PLANE
FIRST = LONG + PLANE
KEPT = SENT + PLANE

CORE = [(i, i ^ 1) for i in range(N_ROW)]
X_HI = [(i, i ^ 1) for i in range(N_COL)]
ACROSS = [(i, (i - 1 + 2 * (i % 2)) % N_COL) for i in range(N_COL)]
X_LO = [(i, i ^ 2) for i in range(N_ROW)]
RING = [(i, (i + (QUAD if i % 2 == 0 else -QUAD)) % N_ROW) for i in range(N_ROW)]

CHAINS = ((2, 0), (3, 1))
QUADS = [[QUAD * z + q for q in range(QUAD)] for z in range(N_Z)]
MINE = [(0, steps) for steps in range(1, 5)] + [(1, steps) for steps in range(1, 4)]
PIECES = MINE + [(1 - flip, -steps) for flip, steps in MINE]

EARLY = [(flip, steps) for flip, steps in PIECES if abs(steps) < 4]

ANY = pl.BlockSpec(memory_space=pl.ANY)
VMEM = pl.BlockSpec(memory_space=pltpu.VMEM)
SMEM = pl.BlockSpec(memory_space=pltpu.SMEM)


def over_row(value, pairs):
    return lax.ppermute(value, "row", pairs)


def over_col(value, pairs):
    return lax.ppermute(value, "col", pairs)


def after(value, other):
    return lax.optimization_barrier((value, other))[0]


def params():
    return pltpu.CompilerParams(vmem_limit_bytes=20 * 2**20)


def forward_kernel(place, rows, cols, count, tiles, plane, *rest):
    pieces, (total, wide, near, far, late, field, sems) = rest[: len(EARLY)], rest[len(EARLY) :]
    z = place[0]
    quad = place[1]
    core = quad & 1
    up = 1 - 2 * core
    copies = [pltpu.make_async_copy(plane, field.at[pl.ds(z * PLANE, PLANE)], sems.at[len(EARLY)])]
    for i, ((flip, steps), piece) in enumerate(zip(EARLY, pieces)):
        from_plane = lax.rem(z - steps * up + 2 * N_Z, N_Z)
        half = core if flip == 0 else 1 - core
        there = field.at[pl.ds(from_plane * PLANE + half * HALF, HALF)]
        copies.append(pltpu.make_async_copy(piece, there, sems.at[i]))
    for copy in copies:
        copy.start()
    for copy in copies:
        copy.wait()
    total[...] = jnp.zeros_like(total)
    used = count[0]

    def group(index, listed):
        terms = []
        for u in range(GROUP):
            slot = index * GROUP + u
            away = lax.rem(cols[slot] // PLANE - z + N_Z, N_Z)
            term = lax.dot_general(
                field[cols[slot]], tiles[slot], (((1,), (1,)), ((), ())), preferred_element_type=F32
            )
            terms.append(jnp.where((slot < used) & (away != 4), term, 0.0))
            late[1 + listed] = slot
            listed = listed + jnp.where((slot < used) & (away == 4), 1, 0)
        for u in range(GROUP):
            total[rows[index * GROUP + u]] += terms[u]
        return listed

    late[0] = lax.fori_loop(0, (used + GROUP - 1) // GROUP, group, jnp.int32(0))
    to_near = jnp.where(place[2] == 0, OWN_X - HALO, 0)
    to_far = OWN_X - HALO - to_near
    for y in range(WIDE_Y):
        line = lax.rem((z * QUAD + quad) * OWN_Y - HALO + y + N_ROW * OWN_Y, N_ROW * OWN_Y) * OWN_X
        wide[y] = field[pl.ds(line, OWN_X)]
        near[y] = field[pl.ds(line + to_near, HALO)]
        far[y] = field[pl.ds(line + to_far, HALO)]


def forward(place, rows, cols, count, tiles, plane, pieces):
    return pl.pallas_call(
        forward_kernel,
        out_shape=[
            jax.ShapeDtypeStruct((RB, CH, NZ), F32),
            jax.ShapeDtypeStruct((WIDE_Y, OWN_X, CH, NZ), BF16),
            jax.ShapeDtypeStruct((WIDE_Y, HALO, CH, NZ), BF16),
            jax.ShapeDtypeStruct((WIDE_Y, HALO, CH, NZ), BF16),
            jax.ShapeDtypeStruct((SLOTS + 1,), jnp.int32),
        ],
        in_specs=[SMEM] * 4 + [VMEM] + [ANY] * (1 + len(pieces)),
        out_specs=[VMEM] * 4 + [SMEM],
        scratch_shapes=[
            pltpu.VMEM((LINES, CH, NZ), BF16),
            pltpu.SemaphoreType.DMA((1 + len(pieces),)),
        ],
        compiler_params=params(),
        cost_estimate=pl.CostEstimate(
            flops=2 * SLOTS * NZ * NZ * CH, bytes_accessed=12 * 2**20, transcendentals=0
        ),
        name="forward_tiles",
    )(place, rows, cols, count, tiles, plane, *pieces)


def late_kernel(place, rows, cols, late, tiles, partial, mine, theirs, out, field, total):
    core = place[1] & 1
    field[pl.ds(core * HALF, HALF)] = mine[...]
    field[pl.ds((1 - core) * HALF, HALF)] = theirs[...]
    total[...] = partial[...]

    def one(index, carry):
        slot = late[1 + index]
        total[rows[slot]] += lax.dot_general(
            field[lax.rem(cols[slot], PLANE)],
            tiles[slot],
            (((1,), (1,)), ((), ())),
            preferred_element_type=F32,
        )
        return carry

    lax.fori_loop(0, late[0], one, 0)
    out[...] = total[...].astype(BF16)


def forward_late(place, rows, cols, late, tiles, partial, mine, theirs):
    return pl.pallas_call(
        late_kernel,
        out_shape=jax.ShapeDtypeStruct((RB, CH, NZ), BF16),
        in_specs=[SMEM] * 4 + [VMEM] * 4,
        out_specs=VMEM,
        scratch_shapes=[pltpu.VMEM((PLANE, CH, NZ), BF16), pltpu.VMEM((RB, CH, NZ), F32)],
        compiler_params=params(),
        cost_estimate=pl.CostEstimate(flops=2**24, bytes_accessed=2**21, transcendentals=0),
        name="forward_late_tiles",
    )(place, rows, cols, late, tiles, partial, mine, theirs)


def adjoint_kernel(
    place, rows, cols, count, tiles, observed, weight, *rest
):
    parts, (soon, later, kept, residual, total, first) = rest[:4], rest[4:]
    z = place[0]
    quad = place[1]
    core = quad & 1
    used = count[0]
    for b in range(RB):
        predicted = parts[0][b].astype(F32)
        for part in parts[1:]:
            predicted = predicted + part[b].astype(F32)
        residual[b] = (weight[pl.ds(b, 1), :] * (predicted - observed[pl.ds(b, 1), :])).astype(BF16)
    total[...] = jnp.zeros_like(total)
    soon[...] = jnp.zeros_like(soon)
    later[...] = jnp.zeros_like(later)
    kept[...] = jnp.zeros_like(kept)

    def mark(index, carry):
        slot = used - 1 - index
        first[cols[slot]] = slot
        return carry

    lax.fori_loop(0, used, mark, 0)
    groups = (used + GROUP - 1) // GROUP

    def group(index, carry):
        terms = []
        for u in range(GROUP):
            slot = index * GROUP + u
            terms.append(
                lax.dot_general(
                    residual[rows[slot]], tiles[slot], (((1,), (0,)), ((), ())), preferred_element_type=F32
                )
            )
        for u in range(GROUP):
            slot = index * GROUP + u
            total[jnp.where(slot < used, first[cols[slot]], SLOTS)] += terms[u]
        return carry

    lax.fori_loop(0, groups, group, 0)

    def place_line(slot):
        line = cols[slot]
        away = lax.rem(line // PLANE - z + N_Z, N_Z)
        other = lax.rem(line // OWN, QUAD)
        inner = lax.rem(line, OWN)
        carrier = jnp.where(away == 4, other & 1, jnp.where(away < 4, 0, 1))
        steps = jnp.where(carrier == 0, away, N_Z - away)
        across = 1 - ((other // 2) ^ (quad // 2))
        where = (2 * ((other & 1) ^ carrier) + across) * OWN + inner
        where = jnp.where(steps == 4, 0, LONG + (3 - steps) * PLANE) + where
        near = SENT + (2 * ((other & 1) ^ core) + across) * OWN + inner
        here = (away == 0) | (carrier == core)
        good = slot < used
        value = total[jnp.where(good, first[line], SLOTS)].astype(BF16)
        kept[jnp.where(good & here, jnp.where(away == 0, near, where), KEPT)] = value
        soon[jnp.where(good & ~here & (where < FIRST), where, FIRST)] = value
        later[jnp.where(good & ~here & (where >= FIRST), where - FIRST, SENT - FIRST)] = value

    def place_group(index, carry):
        for u in range(GROUP):
            place_line(index * GROUP + u)
        return carry

    lax.fori_loop(0, groups, place_group, 0)


def adjoint(place, rows, cols, count, tiles, observed, weight, parts):
    return pl.pallas_call(
        adjoint_kernel,
        out_shape=[
            jax.ShapeDtypeStruct((FIRST + 1, CH, NZ), BF16),
            jax.ShapeDtypeStruct((SENT - FIRST + 1, CH, NZ), BF16),
            jax.ShapeDtypeStruct((KEPT + 1, CH, NZ), BF16),
        ],
        in_specs=[SMEM] * 4 + [VMEM] * (3 + len(parts)),
        out_specs=[VMEM] * 3,
        scratch_shapes=[
            pltpu.VMEM((RB, CH, NZ), BF16),
            pltpu.VMEM((SLOTS + 1, CH, NZ), F32),
            pltpu.SMEM((LINES,), jnp.int32),
        ],
        compiler_params=params(),
        cost_estimate=pl.CostEstimate(
            flops=2 * SLOTS * NZ * NZ * CH, bytes_accessed=12 * 2**20, transcendentals=0
        ),
        name="adjoint_tiles",
    )(place, rows, cols, count, tiles, observed, weight, *parts)


def prox_kernel(start, wide, near, far, anchor, noise, out, field, primal, dual_y, dual_x, dual_z):
    y0 = start[0]
    x0 = start[1]
    above = jnp.where(start[2] == 0, HALO + OWN_X, 0)
    below = HALO + OWN_X - above
    lane = lax.broadcasted_iota(jnp.int32, (CH, NZ), 1)
    not_first = lane > 0
    not_last = lane < NZ - 1

    def load_line(y, carry):
        for x in range(OWN_X):
            field[y, HALO + x] = wide[y, x].astype(F32)
        for x in range(HALO):
            field[y, above + x] = near[y, x].astype(F32)
            field[y, below + x] = far[y, x].astype(F32)
        return carry

    lax.fori_loop(0, WIDE_Y, load_line, 0)
    for y in range(OWN_Y):
        for x in range(OWN_X):
            field[HALO + y, HALO + x] = anchor[y, x]

    def primal_at(y, x):
        along_z = dual_z[y, x]
        lower_z = jnp.where(not_first, pltpu.roll(along_z, 1, 1), 0.0)
        term = (dual_y[y - 1, x] - dual_y[y, x]) + (dual_x[y, x - 1] - dual_x[y, x]) + (lower_z - along_z)
        return field[y, x] - theta_tv * term

    for step in range(3):
        source = field if step == 0 else primal
        if step:

            def primal_line(y, carry, step=step):
                for x in range(step, WIDE_X - step):
                    primal[y, x] = primal_at(y, x)
                return carry

            lax.fori_loop(step, WIDE_Y - step, primal_line, 0)

        def dual_line(y, carry, step=step, source=source):
            line = y0 + y
            rate_y = jnp.where((line >= 0) & (line < TOP_Y), tau_dual, 0.0)
            for x in range(step, WIDE_X - 1 - step):
                plane = x0 + x
                rate_x = jnp.where((plane >= 0) & (plane < TOP_X), tau_dual, 0.0)
                here = source[y, x]
                diff_y = rate_y * (source[y + 1, x] - here)
                diff_x = rate_x * (source[y, x + 1] - here)
                diff_z = jnp.where(not_last, tau_dual * (pltpu.roll(here, NZ - 1, 1) - here), 0.0)
                if step:
                    diff_y = dual_y[y, x] + diff_y
                    diff_x = dual_x[y, x] + diff_x
                    diff_z = dual_z[y, x] + diff_z
                dual_y[y, x] = jnp.clip(diff_y, -1.0, 1.0)
                dual_x[y, x] = jnp.clip(diff_x, -1.0, 1.0)
                dual_z[y, x] = jnp.clip(diff_z, -1.0, 1.0)
            return carry

        lax.fori_loop(step, WIDE_Y - 1 - step, dual_line, 0)
    for y in range(OWN_Y):
        for x in range(OWN_X):
            here = field[HALO + y, HALO + x]
            prox = primal_at(HALO + y, HALO + x)
            out[y, x] = here - step_size / moreau * (here - prox) + noise_scale * noise[y, x]


def prox_step(start, wide, near, far, anchor, noise):
    region = pltpu.VMEM((WIDE_Y, WIDE_X, CH, NZ), F32)
    return pl.pallas_call(
        prox_kernel,
        out_shape=jax.ShapeDtypeStruct((OWN_Y, OWN_X, CH, NZ), F32),
        in_specs=[SMEM] + [VMEM] * 5,
        out_specs=VMEM,
        scratch_shapes=[region] * 5,
        compiler_params=params(),
        cost_estimate=pl.CostEstimate(flops=2**24, bytes_accessed=12 * 2**20, transcendentals=0),
        name="tv_prox",
    )(start, wide, near, far, anchor, noise)


def own_half(value, pick):
    half = value.shape[0] // 2
    return jnp.where(pick == 0, value[:half], value[half:])


def gather_slab(own, core):
    plane = lax.all_gather(own, "row", axis=0, tiled=True, axis_index_groups=QUADS)
    chains = [own_half(plane, core), own_half(plane, 1 - core)]
    mine = {}
    for steps in range(1, 5):
        for flip in range(2 if steps < 4 else 1):
            chains[flip] = over_row(chains[flip], RING)
            mine[flip, steps] = chains[flip]
    early = [key for key in MINE if key[1] < 4]
    theirs = [over_row(mine[key], CORE) for key in early]
    return plane, [mine[key] for key in early] + theirs, mine[0, 4]


def add(*parts):
    total = parts[0].astype(F32)
    for part in parts[1:]:
        total = total + part.astype(F32)
    return total.astype(BF16)


def scatter_gradient(soon, later, kept, chains, beside):
    came_soon = over_row(soon, CORE)
    came_later = over_row(later, CORE)
    turns = {2: 0, 0: 1, 3: 2, 1: 3}

    def chip(steps, sides, *more):
        start = (0 if steps == 4 else LONG + (3 - steps) * PLANE) + turns[sides[0]] * OWN
        size = len(sides) * OWN
        came = came_soon if start < FIRST else came_later
        first = start if start < FIRST else start - FIRST
        return add(kept[start : start + size], came[first : first + size], *more)

    ring = {}
    sent = []
    last = None
    long, short = chains
    for steps, sides in ((4, long), (3, short), (3, long), (2, short), (2, long), (1, short), (1, long)):
        more = [after(ring[sides], last)] if sides in ring else []
        last = chip(steps, sides, *more)
        sent.append(last)
        ring[sides] = over_row(last, RING)

    def terms(sides, side, *order):
        at = sides.index(side) * OWN
        own = SENT + turns[side] * OWN
        brought = after(ring[sides], order) if order else ring[sides]
        return brought[at : at + OWN], kept[own : own + OWN]

    give = add(*terms(short, 3, last))
    other = add(*terms(short, 1, give), over_row(give, X_LO))
    result = beside(sent[2], last)
    give = add(*terms(long, 2, give, result))
    got = over_row(give, X_LO)
    return [*terms(long, 0, give), got, over_row(other, CORE)], result


def body(x_state, langevin_noise, observed, data_weight, sens_tiles, tile_rows, tile_cols, counts):
    row = lax.axis_index("row")
    col = lax.axis_index("col")
    place = jnp.stack([row // QUAD, row % QUAD, col % 2]).astype(jnp.int32)
    start = jnp.stack([row * OWN_Y - HALO, col * OWN_X - HALO, col % 2]).astype(jnp.int32)
    state = x_state.transpose(0, 1, 3, 2)
    noise = langevin_noise.transpose(0, 1, 3, 2)
    own = after(state, (place, start)).reshape(OWN, CH, NZ).astype(BF16)
    tiles = sens_tiles[0, 0]
    rows, cols, count = tile_rows[0, 0], tile_cols[0, 0], counts[0]

    plane, early, mine = gather_slab(own, row % 2)
    partial, wide, to_near, to_far, late = forward(place, rows, cols, count, tiles, plane, early)
    mine = after(mine, partial)
    part = forward_late(place, rows, cols, late, tiles, partial, mine, over_row(mine, CORE))
    came = over_col(part, X_HI)
    near = over_col(to_near, X_HI)
    part = add(part, came)
    parts = [part] + [
        over_col(part, [(i, (i + by) % N_COL) for i in range(N_COL)]) for by in (2, 4, 6)
    ]
    parts[0] = after(part, near)
    soon, later, kept = adjoint(
        place,
        rows,
        cols,
        count,
        tiles,
        observed.reshape(RB, NZ),
        data_weight.reshape(RB, NZ),
        parts,
    )
    def beside(early, last):
        far = over_col(after(to_far, early), ACROSS)
        return prox_step(start, wide, after(near, last), far, state, noise)

    terms, base = scatter_gradient(soon, later, kept, CHAINS, beside)
    gradient = sum(v.astype(F32) for v in terms)
    out = base - step_size * gradient.reshape(OWN_Y, OWN_X, CH, NZ)
    return out.transpose(0, 1, 3, 2)


def solution(mesh):
    placed = (
        P("row", "col", None, None),
        P("row", "col", None, None),
        P("row"),
        P("row"),
        P("row", "col", None, None, None),
        P("row", "col", None),
        P("row", "col", None),
        P("row", "col"),
    )
    return jax.shard_map(
        body, mesh=mesh, in_specs=placed, out_specs=P("row", "col", None, None), check_vma=False
    )
```
